1024 devices in a mesh: dp: 16 (over x, y), expert: 64 (over z, core).
Axes of the slice: x: 4, y: 4, z: 32, core: 2. Of those that a mesh axis runs over, the one named last changes fastest.
Arguments:
- tokens: bfloat16 [1024, 7168], P('expert', 'dp'), may hold values from -6 to 6
- expert_ids: int32 [1024, 8], P('expert'), may hold values from 0 to 63, all different within a row; in each aligned block of 16 rows (0 to 15, 16 to 31, ...) at most 4 rows name the same one
- gate_weights: float32 [1024, 8], P('expert'), may hold values from 0.05 to 0.5
- response_mask: int32 [1024], P('expert'), may hold values 0 or 1
- cotangent: bfloat16 [1024, 7168], P('expert', 'dp'), may hold values from -6 to 6
- w_gate: bfloat16 [64, 7168, 1024], P('expert', 'dp'), may hold values from -0.0625 to 0.0625
- w_up: bfloat16 [64, 7168, 1024], P('expert', 'dp'), may hold values from -0.0625 to 0.0625
- w_down: bfloat16 [64, 1024, 7168], P('expert', None, 'dp'), may hold values from -0.1875 to 0.1875
- shared_gate: bfloat16 [7168, 2048], P('dp'), may hold values from -0.0625 to 0.0625
- shared_up: bfloat16 [7168, 2048], P('dp'), may hold values from -0.0625 to 0.0625
- shared_down: bfloat16 [2048, 7168], P(None, 'dp'), may hold values from -0.125 to 0.125
Outputs:
- mixed: bfloat16 [1024, 7168], P('expert', 'dp')
- token_grad: bfloat16 [1024, 7168], P('expert', 'dp')
- gate_grad: float32 [1024, 8], P('expert')
The draws below stay inside these ranges and needn't reach their ends.
Inputs may be any that keep to these rules, and one draw needn't show every extreme that they name: `expert_ids`: each row names 8 different experts; in each aligned block of 16 rows (the rows of one device) no expert is named by more than 4 rows.
All inputs are finite; a program needn't handle non-finite values. No bound on the sum of `response_mask` on one device may be relied on, other than what follows from the above.
Results may differ from the reference program's by a relative error of at most 0.039.
Values may be sent and summed in bfloat16 or wider, within the bound.
A program may use at most 32 MiB of HBM per device.

```python
import math
import jax
import jax.numpy as jnp
import numpy as np
from jax import lax

D = 7168
F = 1024
FS = 2048
TOP = 8
TOK_DEV = 16
EXPERTS = 64
CAP = 4
TOKENS = 1024
N_DP = 16
N_EXPERT = 64


def plant(entries, rng, smallest, largest):
    index_at = [jax.random.randint(jax.random.fold_in(rng, axis), (), 0, length) for axis, length in enumerate(entries.shape)]
    widest = entries.shape.index(max(entries.shape))
    neighbour = index_at[:widest] + [(index_at[widest] + 1) % entries.shape[widest]] + index_at[widest + 1:]
    return entries.at[tuple(index_at)].set(smallest).at[tuple(neighbour)].set(largest)


def block_levels(own_key, shape, split, least, largest):
    def one(dim, shards_of):
        draws = jax.random.uniform(jax.random.fold_in(jax.random.fold_in(own_key, 6), dim), (shards_of,), jnp.float32, least / len(split), largest / len(split))
        return jnp.repeat(jnp.exp(draws), shape[dim] // shards_of).reshape((-1,) + (1,) * (len(shape) - dim - 1))

    level = one(*split[0])
    for cut in split[1:]:
        level = level * one(*cut)
    return level


def deal_out(rng, own, number, rows, number_of, top, most, skew):
    ranking = jax.random.permutation(rng, number_of)
    heavy_load, usual = portions_of(number_of, rows * top, most, skew, True), portions_of(number_of, rows * top, most, skew, False)
    places = jnp.arange(number_of)

    def named(lengths, offset_by):
        used = int((lengths > 0).sum())
        fixed = max(1, used // 4)
        moved = fixed + (places - fixed + offset_by * (used - fixed)) % max(1, number_of - fixed)
        return jnp.zeros((number_of,), jnp.int32).at[ranking[jnp.where(places < fixed, places, moved)]].set(jnp.asarray(lengths, jnp.int32))

    lengths = jnp.where(number % 4 == 0, named(heavy_load, number // 4), named(usual, number - number // 4 - 1))
    mixed = jax.random.permutation(jax.random.fold_in(own, 3), number_of)
    source_of, taker = mixed[0:number_of // 2 * 2:2], mixed[1:number_of // 2 * 2:2]
    slack = jnp.minimum(lengths[source_of] - 1, most - lengths[taker]) // 2
    slack = jnp.where((source_of == ranking[0]) | (taker == ranking[0]) | (lengths[taker] == 0), 0, jnp.maximum(slack, 0))
    moved = jax.random.randint(jax.random.fold_in(own, 4), (number_of // 2,), 0, 1 << 20) % (slack + 1)
    lengths = lengths.at[source_of].add(-moved).at[taker].add(moved)
    items = jnp.searchsorted(jnp.cumsum(lengths), jnp.arange(rows * top), side="right").astype(jnp.int32)
    listing = items.reshape(top, rows).T
    listing = listing[jax.random.permutation(jax.random.fold_in(own, 1), rows)]
    offset_by = jax.random.randint(jax.random.fold_in(own, 2), (rows, 1), 0, top)
    return jnp.take_along_axis(listing, (jnp.arange(top)[None, :] + offset_by) % top, axis=1)


def portions_of(number_of, total, reach, skew, full):
    weights = [(1 << 20) // math.isqrt(grade ** skew) + 1 for grade in range(1, number_of + 1)]
    largest = reach if full else min(reach, max(-(-total // number_of), total * weights[0] // sum(weights)))
    least = 1 if total - largest >= number_of - 1 else 0
    given, surplus = [largest] + [least] * (number_of - 1), total - largest - least * (number_of - 1)
    while surplus > 0:
        free = [i for i in range(1, number_of) if given[i] < largest] or [i for i in range(1, number_of) if given[i] < reach]
        pool, remaining = sum([weights[i] for i in free]), surplus
        for i in free:
            extra = min(reach - given[i], max(1, remaining * weights[i] // pool), surplus)
            given[i] = given[i] + extra
            surplus = surplus - extra
    return np.array(given)


def bell_draw(rng, dims, spread, most, shards=(), kind=jnp.bfloat16):
    array = jax.random.normal(rng, dims, jnp.float32) * spread
    if len(shards) > 0:
        array = block_levels(rng, dims, shards, -0.22, 0.18) * array
    return jnp.clip(array, min=-most, max=most).astype(kind)


def setup_inputs(seed: int = 0) -> dict:
    seeds = jax.random.split(jax.random.key(seed), 12)
    tokens = bell_draw(seeds[0], (TOKENS, D), 1.0, 6.0, ((0, 64), (1, 16)))
    expert_ids_keys = jax.random.split(jax.random.fold_in(seeds[1], 1), TOKENS // TOK_DEV)
    expert_ids_turns = jax.random.permutation(jax.random.fold_in(seeds[1], 3), TOKENS // TOK_DEV)
    expert_ids = jax.vmap(lambda own, number: deal_out(jax.random.fold_in(seeds[1], 2), own, number, TOK_DEV, EXPERTS, TOP, CAP, 2))(expert_ids_keys, expert_ids_turns).reshape((TOKENS, TOP))
    gate_weights = jnp.clip(jnp.exp(math.log(0.5) - 2.3025851 * jax.random.uniform(seeds[2], (TOKENS, TOP), jnp.float32) ** block_levels(seeds[2], (TOKENS, TOP), ((0, 64),), -0.2, 0.2)), 0.05, 0.5)
    response_mask = plant((jax.random.randint(seeds[3], (TOKENS,), 0, 4) < 3).astype(jnp.int32), jax.random.fold_in(seeds[3], 1), 0, 1)
    cotangent = bell_draw(seeds[4], (TOKENS, D), 1.0, 6.0, ((0, 64), (1, 16)))
    w_gate = bell_draw(seeds[5], (EXPERTS, D, F), D ** -0.5, 0.0625, ((0, 64), (1, 16)))
    w_up = bell_draw(seeds[6], (EXPERTS, D, F), D ** -0.5, 0.0625, ((0, 64), (1, 16)))
    w_down = bell_draw(seeds[7], (EXPERTS, F, D), F ** -0.5, 0.1875, ((0, 64), (2, 16)))
    shared_gate = bell_draw(seeds[8], (D, FS), D ** -0.5, 0.0625, ((0, 16),))
    shared_up = bell_draw(seeds[9], (D, FS), D ** -0.5, 0.0625, ((0, 16),))
    shared_down = bell_draw(seeds[10], (FS, D), FS ** -0.5, 0.125, ((1, 16),))
    return {"tokens": tokens, "expert_ids": expert_ids, "gate_weights": gate_weights, "response_mask": response_mask, "cotangent": cotangent, "w_gate": w_gate, "w_up": w_up, "w_down": w_down, "shared_gate": shared_gate, "shared_up": shared_up, "shared_down": shared_down}


def silu_pair(gate_part, up_part):
    sigma = jax.nn.sigmoid(gate_part)
    return gate_part * sigma * up_part


def silu_back(grad_hidden, gate_part, up_part):
    sigma = jax.nn.sigmoid(gate_part)
    grad_gate = grad_hidden * up_part * sigma * (1.0 + gate_part * (1.0 - sigma))
    grad_up = grad_hidden * gate_part * sigma
    return grad_gate.astype(jnp.bfloat16), grad_up.astype(jnp.bfloat16)


def split_sum(left, right):
    group = left.shape[1] // N_DP
    total = jnp.zeros((left.shape[0], right.shape[1]), jnp.float32)
    for piece in range(N_DP):
        term = jnp.dot(left[:, piece * group:(piece + 1) * group], right[piece * group:(piece + 1) * group], preferred_element_type=jnp.float32)
        total = total + lax.optimization_barrier(term.astype(jnp.bfloat16)).astype(jnp.float32)
    return total


def placements(expert_ids):
    blocks = expert_ids.reshape(N_EXPERT, TOK_DEV * TOP).astype(jnp.int32)
    onehot = (blocks[:, :, None] == jnp.arange(EXPERTS, dtype=jnp.int32)[None, None, :]).astype(jnp.int32)
    earlier = (jnp.cumsum(onehot, axis=1) - onehot).astype(jnp.int32)
    position = jnp.sum(onehot * earlier, axis=2).astype(jnp.int32)
    source = jnp.arange(N_EXPERT, dtype=jnp.int32)[:, None]
    target = blocks * (N_EXPERT * CAP) + source * CAP + position
    return target.reshape(-1).astype(jnp.int32)


def reference(tokens, expert_ids, gate_weights, response_mask, cotangent, w_gate, w_up, w_down, shared_gate, shared_up, shared_down):
    rows_each = N_EXPERT * CAP
    pair_count = TOKENS * TOP
    target = placements(expert_ids)
    table = jnp.full((EXPERTS * rows_each,), pair_count, jnp.int32)
    table = table.at[target].set(jnp.arange(pair_count, dtype=jnp.int32)).reshape(EXPERTS, rows_each)
    grad_out = (cotangent.astype(jnp.float32) * response_mask.astype(jnp.float32)[:, None]).astype(jnp.bfloat16)
    flat_weights = gate_weights.reshape(-1)

    def one_expert(index):
        entry = table[index]
        valid = entry < pair_count
        safe_entry = jnp.where(valid, entry, 0).astype(jnp.int32)
        token = (safe_entry // TOP).astype(jnp.int32)
        rows = jnp.where(valid[:, None], tokens[token], jnp.zeros((), jnp.bfloat16))
        weight = jnp.where(valid, flat_weights[safe_entry], jnp.zeros((), jnp.float32))
        gate_part = split_sum(rows, w_gate[index])
        up_part = split_sum(rows, w_up[index])
        hidden = silu_pair(gate_part, up_part).astype(jnp.bfloat16)
        output = jnp.dot(hidden, w_down[index], preferred_element_type=jnp.float32).astype(jnp.bfloat16)
        pair_grad = (weight[:, None] * grad_out[token].astype(jnp.float32)).astype(jnp.bfloat16)
        grad_hidden = split_sum(pair_grad, w_down[index].T)
        grad_gate, grad_up = silu_back(grad_hidden, gate_part, up_part)
        row_grad = jnp.dot(grad_gate, w_gate[index].T, preferred_element_type=jnp.float32)
        row_grad = (row_grad + jnp.dot(grad_up, w_up[index].T, preferred_element_type=jnp.float32)).astype(jnp.bfloat16)
        return output, row_grad

    outputs, row_grads = lax.map(one_expert, jnp.arange(EXPERTS, dtype=jnp.int32))
    routed = outputs.reshape(EXPERTS * rows_each, D)[target].reshape(TOKENS, TOP, D).astype(jnp.float32)
    shared_gate_part = split_sum(tokens, shared_gate)
    shared_up_part = split_sum(tokens, shared_up)
    shared_hidden = silu_pair(shared_gate_part, shared_up_part).astype(jnp.bfloat16)
    shared_out = jnp.dot(shared_hidden, shared_down, preferred_element_type=jnp.float32)
    mixed = (shared_out + jnp.sum(gate_weights[:, :, None] * routed, axis=1)).astype(jnp.bfloat16)
    gate_grad = jnp.sum(routed * grad_out.astype(jnp.float32)[:, None, :], axis=2)
    shared_grad_hidden = split_sum(grad_out, shared_down.T)
    shared_grad_gate, shared_grad_up = silu_back(shared_grad_hidden, shared_gate_part, shared_up_part)
    shared_in = jnp.dot(shared_grad_gate, shared_gate.T, preferred_element_type=jnp.float32)
    shared_in = shared_in + jnp.dot(shared_grad_up, shared_up.T, preferred_element_type=jnp.float32)
    back_pairs = row_grads.reshape(EXPERTS * rows_each, D)[target].reshape(TOKENS, TOP, D).astype(jnp.float32)
    token_grad = (shared_in + jnp.sum(back_pairs, axis=1)).astype(jnp.bfloat16)
    return mixed, token_grad, gate_grad
```

```python
import functools

import jax
import jax.numpy as jnp
from jax import lax
from jax.experimental import pallas as pl
from jax.experimental.pallas import tpu as pltpu
from jax.sharding import PartitionSpec as P

MESH = pl.DeviceIdType.MESH
BF = jnp.bfloat16
F32 = jnp.float32
NX, NY, NZ = 4, 4, 32
PEERS = NX * NY
CHUNKS = 4
CAP = 4
TOK = 16
TOP = 8
WIDE = 1024
GRAD = 512
META = 384

TREE_LONG = {0: (4, 2, 1), 4: (8, 6, 5, 3), 8: (12, 10, 9, 7), 12: (16, 15, 14, 13, 11)}
TREE_SHORT = {0: (4, 2, 1), 4: (8, 6, 5, 3), 8: (12, 10, 9, 7), 12: (15, 14, 13, 11)}
TREES = (TREE_LONG, TREE_SHORT)
PARENTS = tuple({k: p for p, ch in t.items() for k in ch} for t in TREES)
HOPS = (1, 2, 3, 4)
SLOTS = (
    ((0, 0), (0, 1), (0, 2), (1, 1), (1, 2), (0, 4), (1, 4), (0, 3)),
    ((1, 3), (0, 5), (1, 5), (0, 6), (1, 6), (0, 8), (1, 8), (0, 7)),
    ((1, 7), (0, 9), (1, 9), (0, 10), (1, 10), (0, 12), (1, 12), (0, 11)),
    ((1, 11), (0, 13), (1, 13), (0, 14), (1, 14), (0, 15), (1, 15), (0, 16)),
)
PLACE = {key: (j, i) for j, row in enumerate(SLOTS) for i, key in enumerate(row)}


def flat(key):
    j, i = PLACE[key]
    return j * 8 + i


def dot(a, b):
    return lax.dot_general(a, b, (((1,), (0,)), ((), ())), preferred_element_type=F32)


def dot_t(a, b):
    return lax.dot_general(a, b, (((1,), (1,)), ((), ())), preferred_element_type=F32)


def kernel(
    tokens, ids, weights, mask, cot, wg_hbm, wu_hbm, wd_hbm, sg_hbm, su_hbm, sd_hbm,
    mixed, token_grad, gate_grad,
    wg, wu, wd, sg, su, sd,
    gath, pick, row_w, row_m, part, got, hid, rout, rsib, comb, back_out, back_in,
    s_part, s_got, s_hid, s_out,
    ld_sem, zs, zr, bs, br, rs_s, rs_r, ag_s, ag_r, ro_s, ro_r, rt_s, rt_r,
):
    dp = lax.axis_index("dp")
    ex = lax.axis_index("expert")
    z = ex // 2
    c = ex % 2
    px = dp // NY
    py = dp % NY
    sign = (1 - 2 * c, 2 * c - 1)

    def z_dev(dz):
        return (dp, lax.rem(z + dz + NZ, NZ) * 2 + c)

    sib = (dp, z * 2 + 1 - c)

    def peer(i):
        tx = lax.rem(px + i // NY, NX)
        ty = lax.rem(py + i % NY, NY)
        return tx, ty

    def peer_dev(i):
        tx, ty = peer(i)
        return (tx * NY + ty, ex)

    def remote(src, dst, ss, rs, dev):
        return pltpu.make_async_remote_copy(
            src_ref=src, dst_ref=dst, send_sem=ss, recv_sem=rs, device_id=dev, device_id_type=MESH
        )

    loads = [
        pltpu.make_async_copy(src, dst, ld_sem.at[n])
        for n, (src, dst) in enumerate(
            ((sg_hbm, sg), (su_hbm, su), (sd_hbm, sd), (wg_hbm, wg), (wu_hbm, wu), (wd_hbm, wd))
        )
    ]
    for load in loads:
        load.start()

    barrier = pltpu.get_barrier_semaphore()
    pl.semaphore_signal(barrier, inc=1, device_id=sib, device_id_type=MESH)
    for h in HOPS:
        pl.semaphore_signal(barrier, inc=1, device_id=z_dev(h), device_id_type=MESH)
        pl.semaphore_signal(barrier, inc=1, device_id=z_dev(-h), device_id_type=MESH)

    def greet(i, carry):
        pl.semaphore_signal(barrier, inc=1, device_id=peer_dev(i), device_id_type=MESH)
        return carry

    lax.fori_loop(1, PEERS, greet, 0)

    lane = lax.broadcasted_iota(jnp.int32, (8, 128), 1)
    row = lax.broadcasted_iota(jnp.int32, (8, 128), 0)

    def spread(at):
        return jnp.where(lane == row + at, 1.0, 0.0).astype(BF)

    w_hi = weights[...].astype(BF)
    w_lo = (weights[...] - w_hi.astype(F32)).astype(BF)
    ids_b = ids[...].astype(F32).astype(BF)
    meta = dot(ids_b, spread(64) + spread(72)) + dot(w_hi, spread(80)) + dot(w_lo, spread(88))
    grad = (cot[...].astype(F32) * mask[...].astype(F32)).astype(BF)
    own = gath.at[0, c, 0]
    own[...] = jnp.zeros((TOK, WIDE), BF)
    own[:, 0:448] = tokens[...]
    own[:, META:512] = (own[:, META:512].astype(F32) + meta).astype(BF)
    own[:, GRAD : GRAD + 448] = grad
    rout[...] = jnp.zeros(rout.shape, BF)

    pl.semaphore_wait(barrier, PEERS + 2 * len(HOPS))

    def z_copy(key, child):
        j, i = PLACE[key]
        jj, ii = PLACE[child]
        n = flat(child)
        d, k = child
        return remote(
            gath.at[j, c, i], gath.at[jj, c, ii], zs.at[n], zr.at[n], z_dev(sign[d] * (k - key[1]))
        )

    def forward(d, p):
        for k in TREES[d].get(p, ()):
            z_copy((0, 0) if p == 0 else (d, p), (d, k)).start()

    def arrive(key):
        d, k = key
        p = PARENTS[d][k]
        z_copy((0, 0) if p == 0 else (d, p), key).wait_recv()
        forward(d, k)

    def sib_copy(j):
        return remote(gath.at[j, c], gath.at[j, c], bs.at[j], br.at[j], sib)

    def relay_in(k):
        arrive((0, k))
        arrive((1, k))

    def stage_d(j):
        for d, k in SLOTS[j]:
            if k in (0, 4, 8, 12):
                continue
            arrive((d, k))
        sib_copy(j).start()

    tok_row = lax.broadcasted_iota(jnp.int32, (128, 128), 0)
    tok_lane = lax.broadcasted_iota(jnp.int32, (128, 128), 1)
    lower = jnp.where((tok_lane < tok_row) & (tok_lane // TOK == tok_row // TOK), 1.0, 0.0).astype(BF)
    ones = jnp.ones((128, 128), BF)
    base = (tok_row // TOK) * CAP

    def selector(meta_f, expert, at):
        match = (tok_lane >= 64) & (tok_lane < 72) & (meta_f == expert)
        hit = dot(jnp.where(match, 1.0, 0.0).astype(BF), ones)
        pos = dot(lower, hit.astype(BF))
        here = (hit > 0.5) & (tok_lane.astype(F32) == (base + at).astype(F32) + pos)
        return jnp.where(here, 1.0, 0.0)

    e_own = ex.astype(F32)
    e_sib = (z * 2 + 1 - c).astype(F32)
    lane64 = lax.broadcasted_iota(jnp.int32, (64, 128), 1)

    def rs_copy(j, i):
        tx, ty = peer(i)
        return remote(part.at[j, tx, ty], got.at[j, i - 1], rs_s.at[j], rs_r.at[j], peer_dev(i))

    def stage_p(j):
        sib_copy(j).wait_recv()
        toks_c = gath[j, c].reshape(128, WIDE)
        toks_s = gath[j, 1 - c].reshape(128, WIDE)
        meta_c = toks_c[:, META:512].astype(F32)
        meta_s = toks_s[:, META:512].astype(F32)
        sel_c = selector(meta_c, e_own, 0)
        sel_s = selector(meta_s, e_own, 0)
        pick[j] = (sel_c + selector(meta_c, e_sib, 32)).astype(BF)
        rows_c = dot(sel_c.T[0:32].astype(BF), toks_c)
        rows_s = dot(sel_s.T[0:32].astype(BF), toks_s)
        rows = jnp.concatenate((rows_c, rows_s), axis=0)
        rmeta = rows[:, META:512]
        same = rmeta == e_own
        both = pltpu.roll(rmeta, 112, 1) + pltpu.roll(rmeta, 104, 1)
        w = jnp.sum(jnp.where(same & (lane64 >= 64) & (lane64 < 72), both, 0.0), axis=1, keepdims=True)
        row_w[j] = jnp.broadcast_to(w, (64, 128))
        row_m[j] = jnp.where(same & (lane64 >= 64) & (lane64 < 80), 1.0, 0.0)
        rows = rows.astype(BF)
        x = rows[:, 0:448]
        g = rows[:, GRAD : GRAD + 448]
        for n, val in enumerate((dot(x, wg[...]), dot(x, wu[...]), dot_t(g, wd[...]))):
            val = val.astype(BF).reshape(NX, TOK, 1024)
            for u in range(NY):
                part[j, :, u, :, n * 256 : n * 256 + 256] = val[:, :, u * 256 : u * 256 + 256]

        def send(i, carry):
            rs_copy(j, i).start()
            return carry

        lax.fori_loop(1, PEERS, send, 0)

    def ag_copy(j, i):
        mine = hid.at[j, dp]
        return remote(mine, mine, ag_s.at[j], ag_r.at[j], peer_dev(i))

    def activations(gate, up, dh, scale):
        sig = jax.nn.sigmoid(gate)
        h = (gate * sig * up).astype(BF)
        gh = dh if scale is None else dh * scale
        gg = (gh * up * sig * (1.0 + gate * (1.0 - sig))).astype(BF)
        gu = (gh * gate * sig).astype(BF)
        return h, gg, gu

    lane16 = lax.broadcasted_iota(jnp.int32, (TOK, 128), 1)

    def stage_e(j):
        remote(got.at[j], got.at[j], rs_s.at[j], rs_r.at[j], sib).wait_recv()
        acc = part[j, px, py].astype(F32)
        for i in range(PEERS - 1):
            acc = acc + got[j, i].astype(F32)
        gate, up, dh = acc[:, 0:256], acc[:, 256:512], acc[:, 512:768]
        w = row_w[j, pl.ds(pl.multiple_of(px * TOK, TOK), TOK), :][:, 0:1]
        h, gg, gu = activations(gate, up, dh, w)
        s = jnp.sum(h.astype(F32) * dh, axis=1, keepdims=True)
        s_hi = s.astype(BF).astype(F32)
        tail = jnp.where(lane16 == 0, s_hi, jnp.where(lane16 == 1, s - s_hi, 0.0)).astype(BF)
        hid[j, dp] = jnp.concatenate((h, gg, gu, tail), axis=1)

        def send(i, carry):
            ag_copy(j, i).start()
            return carry

        lax.fori_loop(1, PEERS, send, 0)

    def ro_copy(j):
        return remote(rout.at[j, pl.ds(32, 32)], rsib.at[j], ro_s.at[j], ro_r.at[j], sib)

    def stage_m(j):
        many = hid.at[j, pl.ds(0, PEERS - 1)]
        remote(many, many, ag_s.at[j], ag_r.at[j], sib).wait_recv()

        def full(n):
            return jnp.concatenate(
                [
                    jnp.concatenate(
                        [hid[j, r * NY + u, :, n * 256 : n * 256 + 256] for u in range(NY)], axis=1
                    )
                    for r in range(NX)
                ],
                axis=0,
            )

        eo = dot(full(0), wd[...])
        rg = dot_t(full(1), wg[...]) + dot_t(full(2), wu[...])
        tails = []
        for r in range(NX):
            t = hid[j, r * NY, :, 768:896].astype(F32)
            for u in range(1, NY):
                t = t + hid[j, r * NY + u, :, 768:896].astype(F32)
            tails.append(t)
        s = jnp.sum(jnp.concatenate(tails, axis=0), axis=1, keepdims=True)
        s_hi = s.astype(BF).astype(F32)
        extra = row_m[j] * jnp.where(lane64 < 72, s_hi, s - s_hi)
        rout[j, :, 0:448] = (eo * row_w[j][:, 0:1]).astype(BF)
        rout[j, :, META:512] = (rout[j, :, META:512].astype(F32) + extra).astype(BF)
        rout[j, :, GRAD : GRAD + 448] = rg.astype(BF)
        ro_copy(j).start()

    def back_copy(key):
        d, k = key
        n = flat(key)
        p = PARENTS[d][k]
        return remote(
            back_out.at[n], back_in.at[n], rt_s.at[n], rt_r.at[n], z_dev(-sign[d] * (k - p))
        )

    def stage_c(j):
        ro_copy(j).wait_recv()
        both = jnp.concatenate((rout[j, 0:32], rsib[j]), axis=0)
        out = dot(pick[j][:, 0:64], both).reshape(8, TOK, WIDE)
        for i, (d, k) in enumerate(SLOTS[j]):
            if k not in (0, 4, 8, 12):
                back_out[j * 8 + i] = out[i].astype(BF)
                back_copy((d, k)).start()
            else:
                comb[j * 8 + i] = out[i]

    def children_sum(d, p, total):
        for k in TREES[d].get(p, ()):
            back_copy((d, k)).wait_recv()
            total = total + back_in[flat((d, k))].astype(F32)
        return total

    def relay_out(k):
        for d in (0, 1):
            n = flat((d, k))
            back_out[n] = children_sum(d, k, comb[n]).astype(BF)
            back_copy((d, k)).start()

    def sr_copy(i):
        tx, ty = peer(i)
        return remote(s_part.at[tx * NY + ty], s_got.at[i - 1], rs_s.at[CHUNKS], rs_r.at[CHUNKS], peer_dev(i))

    def sa_copy(i):
        mine = s_hid.at[dp]
        return remote(mine, mine, ag_s.at[CHUNKS], ag_r.at[CHUNKS], peer_dev(i))

    def shared_p():
        for n, (x, w, load, mul) in enumerate(
            (
                (tokens[...], sg, loads[0], dot),
                (tokens[...], su, loads[1], dot),
                (own[:, GRAD : GRAD + 448], sd, loads[2], dot_t),
            )
        ):
            load.wait()
            val = mul(x, w[...]).astype(BF)
            for p in range(PEERS):
                s_part[p, :, n * 128 : n * 128 + 128] = val[:, p * 128 : p * 128 + 128]

        def send(i, carry):
            sr_copy(i).start()
            return carry

        lax.fori_loop(1, PEERS, send, 0)

    def shared_e():
        remote(s_got, s_got, rs_s.at[CHUNKS], rs_r.at[CHUNKS], sib).wait_recv()
        acc = s_part[dp].astype(F32)
        for i in range(PEERS - 1):
            acc = acc + s_got[i].astype(F32)
        h, gg, gu = activations(acc[:, 0:128], acc[:, 128:256], acc[:, 256:384], None)
        s_hid[dp] = jnp.concatenate((h, gg, gu), axis=1)

        def send(i, carry):
            sa_copy(i).start()
            return carry

        lax.fori_loop(1, PEERS, send, 0)

    def shared_m():
        many = s_hid.at[pl.ds(0, PEERS - 1)]
        remote(many, many, ag_s.at[CHUNKS], ag_r.at[CHUNKS], sib).wait_recv()

        def full(n):
            return jnp.concatenate([s_hid[p, :, n * 128 : n * 128 + 128] for p in range(PEERS)], axis=1)

        s_out[0] = dot(full(0), sd[...])
        s_out[1] = dot_t(full(1), sg[...]) + dot_t(full(2), su[...])

    forward(0, 0)
    forward(1, 0)
    shared_p()
    for load in loads[3:]:
        load.wait()
    relay_in(4)
    stage_d(0)
    shared_e()
    stage_p(0)
    relay_in(8)
    stage_d(1)
    stage_e(0)
    stage_p(1)
    relay_in(12)
    stage_d(2)
    shared_m()
    stage_e(1)
    stage_p(2)
    stage_m(0)
    stage_d(3)
    stage_e(2)
    stage_p(3)
    stage_c(0)
    stage_m(1)
    stage_m(2)
    stage_c(1)
    stage_e(3)
    stage_c(2)
    stage_m(3)
    stage_c(3)
    relay_out(12)
    relay_out(8)
    relay_out(4)
    total = children_sum(1, 0, children_sum(0, 0, comb[0]))
    mixed[...] = (s_out[0] + total[:, 0:448]).astype(BF)
    token_grad[...] = (s_out[1] + total[:, GRAD : GRAD + 448]).astype(BF)
    tail = total[:, META:512]
    gate_grad[...] = (pltpu.roll(tail, 64, 1) + pltpu.roll(tail, 56, 1))[:, 0:TOP]

    for j in range(CHUNKS):
        for i, key in enumerate(SLOTS[j]):
            if key != (0, 0):
                n = j * 8 + i
                remote(gath.at[0, c, 0], gath.at[0, c, 0], zs.at[n], zr.at[n], sib).wait_send()
                back_copy(key).wait_send()
        sib_copy(j).wait_send()
        ro_copy(j).wait_send()
        remote(got.at[j], got.at[j], rs_s.at[j], rs_r.at[j], sib).wait_send()
        many = hid.at[j, pl.ds(0, PEERS - 1)]
        remote(many, many, ag_s.at[j], ag_r.at[j], sib).wait_send()
    remote(s_got, s_got, rs_s.at[CHUNKS], rs_r.at[CHUNKS], sib).wait_send()
    many = s_hid.at[pl.ds(0, PEERS - 1)]
    remote(many, many, ag_s.at[CHUNKS], ag_r.at[CHUNKS], sib).wait_send()


def on_device(
    tokens, expert_ids, gate_weights, response_mask, cotangent,
    w_gate, w_up, w_down, shared_gate, shared_up, shared_down,
):
    vmem = pl.BlockSpec(memory_space=pltpu.VMEM)
    hbm = pl.BlockSpec(memory_space=pl.ANY)
    width = tokens.shape[1]
    units, shared_units = w_gate.shape[2], shared_gate.shape[1]
    sem = pltpu.SemaphoreType.DMA
    blocks = CHUNKS * 8
    return pl.pallas_call(
        kernel,
        out_shape=(
            jax.ShapeDtypeStruct((TOK, width), BF),
            jax.ShapeDtypeStruct((TOK, width), BF),
            jax.ShapeDtypeStruct((TOK, TOP), F32),
        ),
        in_specs=[vmem] * 5 + [hbm] * 6,
        out_specs=(vmem, vmem, vmem),
        scratch_shapes=[
            pltpu.VMEM((width, units), BF),
            pltpu.VMEM((width, units), BF),
            pltpu.VMEM((units, width), BF),
            pltpu.VMEM((width, shared_units), BF),
            pltpu.VMEM((width, shared_units), BF),
            pltpu.VMEM((shared_units, width), BF),
            pltpu.VMEM((CHUNKS, 2, 8, TOK, WIDE), BF),
            pltpu.VMEM((CHUNKS, 128, 128), BF),
            pltpu.VMEM((CHUNKS, 64, 128), F32),
            pltpu.VMEM((CHUNKS, 64, 128), F32),
            pltpu.VMEM((CHUNKS, NX, NY, TOK, 768), BF),
            pltpu.VMEM((CHUNKS, PEERS - 1, TOK, 768), BF),
            pltpu.VMEM((CHUNKS, PEERS, TOK, 896), BF),
            pltpu.VMEM((CHUNKS, 64, WIDE), BF),
            pltpu.VMEM((CHUNKS, 32, WIDE), BF),
            pltpu.VMEM((blocks, TOK, WIDE), F32),
            pltpu.VMEM((blocks, TOK, WIDE), BF),
            pltpu.VMEM((blocks, TOK, WIDE), BF),
            pltpu.VMEM((PEERS, TOK, 384), BF),
            pltpu.VMEM((PEERS - 1, TOK, 384), BF),
            pltpu.VMEM((PEERS, TOK, 384), BF),
            pltpu.VMEM((2, TOK, width), F32),
            sem((6,)),
            sem((blocks,)),
            sem((blocks,)),
            sem((CHUNKS,)),
            sem((CHUNKS,)),
            sem((CHUNKS + 1,)),
            sem((CHUNKS + 1,)),
            sem((CHUNKS + 1,)),
            sem((CHUNKS + 1,)),
            sem((CHUNKS,)),
            sem((CHUNKS,)),
            sem((blocks,)),
            sem((blocks,)),
        ],
        compiler_params=pltpu.CompilerParams(
            collective_id=0, has_side_effects=True, vmem_limit_bytes=50 << 20
        ),
    )(
        tokens,
        expert_ids,
        gate_weights,
        response_mask.reshape(TOK, 1),
        cotangent,
        w_gate[0],
        w_up[0],
        w_down[0],
        shared_gate,
        shared_up,
        shared_down,
    )


def solution(mesh):
    return jax.shard_map(
        on_device,
        mesh=mesh,
        in_specs=(
            P("expert", "dp"),
            P("expert", None),
            P("expert", None),
            P("expert"),
            P("expert", "dp"),
            P("expert", "dp", None),
            P("expert", "dp", None),
            P("expert", None, "dp"),
            P("dp", None),
            P("dp", None),
            P(None, "dp"),
        ),
        out_specs=(P("expert", "dp"), P("expert", "dp"), P("expert", None)),
        check_vma=False,
    )
```

```python
import functools

import jax
import jax.numpy as jnp
from jax import lax
from jax.experimental import pallas as pl
from jax.experimental.pallas import tpu as pltpu
from jax.sharding import PartitionSpec as P

MESH = pl.DeviceIdType.MESH
BF = jnp.bfloat16
F32 = jnp.float32
NX, NY, NZ = 4, 4, 32
PEERS = NX * NY
CHUNKS = 4
CAP = 4
TOK = 16
TOP = 8
WIDE = 1024
GRAD = 512
META = 384

TREE_LONG = {0: (4, 2, 1), 4: (8, 6, 5, 3), 8: (12, 10, 9, 7), 12: (16, 15, 14, 13, 11)}
TREE_SHORT = {0: (4, 2, 1), 4: (8, 6, 5, 3), 8: (12, 10, 9, 7), 12: (15, 14, 13, 11)}
TREES = (TREE_LONG, TREE_SHORT)
PARENTS = tuple({k: p for p, ch in t.items() for k in ch} for t in TREES)
BACKS = TREES
BACK_PARENTS = tuple({k: p for p, ch in t.items() for k in ch} for t in BACKS)
HOPS = (1, 2, 3, 4)
SLOTS = (
    ((0, 0), (0, 1), (0, 2), (1, 1), (1, 2), (0, 4), (1, 4), (0, 3)),
    ((1, 3), (0, 5), (1, 5), (0, 6), (1, 6), (0, 8), (1, 8), (0, 7)),
    ((1, 7), (0, 9), (1, 9), (0, 10), (1, 10), (0, 12), (1, 12), (0, 11)),
    ((1, 11), (0, 13), (1, 13), (0, 14), (1, 14), (0, 15), (1, 15), (0, 16)),
)
PLACE = {key: (j, i) for j, row in enumerate(SLOTS) for i, key in enumerate(row)}


def flat(key):
    j, i = PLACE[key]
    return j * 8 + i


def dot(a, b):
    return lax.dot_general(a, b, (((1,), (0,)), ((), ())), preferred_element_type=F32)


def dot_t(a, b):
    return lax.dot_general(a, b, (((1,), (1,)), ((), ())), preferred_element_type=F32)


def t_dot(a, b):
    return lax.dot_general(a, b, (((0,), (0,)), ((), ())), preferred_element_type=F32)


def kernel(
    tokens_hbm, ids_hbm, weights_hbm, mask_hbm, cot_hbm, wg_hbm, wu_hbm, wd_hbm, sg_hbm, su_hbm, sd_hbm,
    results,
    tokens, ids, weights, mask, cot, wg, wu, wd, sg, su, sd,
    gath, pick, row_w, row_m, part, got, hid, rout, rsib, comb, back_out, back_in,
    s_part, s_got, s_hid, s_out,
    ld_sem, zs, zr, bs, br, rs_s, rs_r, ag_s, ag_r, ro_s, ro_r, rt_s, rt_r,
):
    dp = lax.axis_index("dp")
    ex = lax.axis_index("expert")
    z = ex // 2
    c = ex % 2
    px = dp // NY
    py = dp % NY
    sign = (1 - 2 * c, 2 * c - 1)

    def z_dev(dz):
        return (dp, lax.rem(z + dz + NZ, NZ) * 2 + c)

    sib = (dp, z * 2 + 1 - c)

    def peer(i):
        tx = lax.rem(px + i // NY, NX)
        ty = lax.rem(py + i % NY, NY)
        return tx, ty

    def peer_dev(i):
        tx, ty = peer(i)
        return (tx * NY + ty, ex)

    def remote(src, dst, ss, rs, dev):
        return pltpu.make_async_remote_copy(
            src_ref=src, dst_ref=dst, send_sem=ss, recv_sem=rs, device_id=dev, device_id_type=MESH
        )

    loads = [
        pltpu.make_async_copy(src, dst, ld_sem.at[n])
        for n, (src, dst) in enumerate(
            (
                (tokens_hbm, tokens), (ids_hbm, ids), (weights_hbm, weights), (mask_hbm, mask), (cot_hbm, cot),
                (sg_hbm, sg), (su_hbm, su), (sd_hbm, sd), (wg_hbm, wg), (wu_hbm, wu), (wd_hbm, wd),
            )
        )
    ]
    for load in loads:
        load.start()
    small, loads = loads[:5], loads[5:]

    barrier = pltpu.get_barrier_semaphore()
    pl.semaphore_signal(barrier, inc=1, device_id=sib, device_id_type=MESH)
    for h in HOPS:
        pl.semaphore_signal(barrier, inc=1, device_id=z_dev(h), device_id_type=MESH)
        pl.semaphore_signal(barrier, inc=1, device_id=z_dev(-h), device_id_type=MESH)

    def greet(i, carry):
        pl.semaphore_signal(barrier, inc=1, device_id=peer_dev(i), device_id_type=MESH)
        return carry

    lax.fori_loop(1, PEERS, greet, 0)

    lane = lax.broadcasted_iota(jnp.int32, (8, 128), 1)
    row = lax.broadcasted_iota(jnp.int32, (8, 128), 0)

    def spread(at):
        return jnp.where(lane == row + at, 1.0, 0.0).astype(BF)

    for load in small:
        load.wait()
    w_hi = weights[...].astype(BF)
    w_lo = (weights[...] - w_hi.astype(F32)).astype(BF)
    ids_b = ids[...].astype(F32).astype(BF)
    meta = t_dot(ids_b, spread(64) + spread(72)) + t_dot(w_hi, spread(80)) + t_dot(w_lo, spread(88))
    eye = lax.broadcasted_iota(jnp.int32, (TOK, TOK), 0) == lax.broadcasted_iota(jnp.int32, (TOK, TOK), 1)
    keep = jnp.where(eye, jnp.broadcast_to(mask[...].astype(F32), (TOK, TOK)), 0.0)
    grad = dot(keep.astype(BF), cot[...]).astype(BF)
    own = gath.at[PLACE[(0, 0)][0], c, PLACE[(0, 0)][1]]
    own[...] = jnp.zeros((TOK, WIDE), BF)
    own[:, 0:448] = tokens[...]
    own[:, META:512] = (own[:, META:512].astype(F32) + meta).astype(BF)
    own[:, GRAD : GRAD + 448] = grad
    rout[...] = jnp.zeros(rout.shape, BF)

    pl.semaphore_wait(barrier, PEERS + 2 * len(HOPS))

    def z_copy(key, child):
        j, i = PLACE[key]
        jj, ii = PLACE[child]
        n = flat(child)
        d, k = child
        return remote(
            gath.at[j, c, i], gath.at[jj, c, ii], zs.at[n], zr.at[n], z_dev(sign[d] * (k - key[1]))
        )

    def forward(d, p):
        for k in TREES[d].get(p, ()):
            z_copy((0, 0) if p == 0 else (d, p), (d, k)).start()

    def arrive(key):
        d, k = key
        p = PARENTS[d][k]
        z_copy((0, 0) if p == 0 else (d, p), key).wait_recv()
        forward(d, k)

    def sib_copy(j):
        return remote(gath.at[j, c], gath.at[j, c], bs.at[j], br.at[j], sib)

    def relay_in(k):
        arrive((0, k))
        arrive((1, k))

    def stage_d(j):
        for d, k in SLOTS[j]:
            if k in (0, 4, 8, 12):
                continue
            arrive((d, k))
        sib_copy(j).start()

    tok_row = lax.broadcasted_iota(jnp.int32, (128, 128), 0)
    tok_lane = lax.broadcasted_iota(jnp.int32, (128, 128), 1)
    lower = jnp.where((tok_lane < tok_row) & (tok_lane // TOK == tok_row // TOK), 1.0, 0.0).astype(BF)
    ones = jnp.ones((128, 128), BF)
    base = (tok_row // TOK) * CAP

    def selector(meta_f, expert, at):
        match = (tok_lane >= 64) & (tok_lane < 72) & (meta_f == expert)
        hit = dot(jnp.where(match, 1.0, 0.0).astype(BF), ones)
        pos = dot(lower, hit.astype(BF))
        here = (hit > 0.5) & (tok_lane.astype(F32) == (base + at).astype(F32) + pos)
        return jnp.where(here, 1.0, 0.0)

    e_own = ex.astype(F32)
    e_sib = (z * 2 + 1 - c).astype(F32)
    lane64 = lax.broadcasted_iota(jnp.int32, (64, 128), 1)

    def rs_copy(j, i):
        tx, ty = peer(i)
        return remote(part.at[j, tx, ty], got.at[j, i - 1], rs_s.at[j], rs_r.at[j], peer_dev(i))

    def stage_p(j):
        sib_copy(j).wait_recv()
        toks_c = gath[j, c].reshape(128, WIDE)
        toks_s = gath[j, 1 - c].reshape(128, WIDE)
        meta_c = toks_c[:, META:512].astype(F32)
        meta_s = toks_s[:, META:512].astype(F32)
        sel_c = selector(meta_c, e_own, 0)
        sel_s = selector(meta_s, e_own, 0)
        pick[j] = (sel_c + selector(meta_c, e_sib, 32)).astype(BF)
        rows_c = dot(sel_c.T[0:32].astype(BF), toks_c)
        rows_s = dot(sel_s.T[0:32].astype(BF), toks_s)
        rows = jnp.concatenate((rows_c, rows_s), axis=0)
        rmeta = rows[:, META:512]
        same = rmeta == e_own
        both = pltpu.roll(rmeta, 112, 1) + pltpu.roll(rmeta, 104, 1)
        w = jnp.sum(jnp.where(same & (lane64 >= 64) & (lane64 < 72), both, 0.0), axis=1, keepdims=True)
        row_w[j] = jnp.broadcast_to(w, (64, 128))
        row_m[j] = jnp.where(same & (lane64 >= 64) & (lane64 < 80), 1.0, 0.0)
        rows = rows.astype(BF)
        x = rows[:, 0:448]
        g = rows[:, GRAD : GRAD + 448]
        for n, val in enumerate((dot(x, wg[...]), dot(x, wu[...]), dot(g, wd[...]))):
            val = val.astype(BF).reshape(NX, TOK, 1024)
            for u in range(NY):
                part[j, :, u, :, n * 256 : n * 256 + 256] = val[:, :, u * 256 : u * 256 + 256]

        def send(i, carry):
            rs_copy(j, i).start()
            return carry

        lax.fori_loop(1, PEERS, send, 0)

    def ag_copy(j, i):
        mine = hid.at[j, dp]
        return remote(mine, mine, ag_s.at[j], ag_r.at[j], peer_dev(i))

    def activations(gate, up, dh, scale):
        sig = jax.nn.sigmoid(gate)
        h = (gate * sig * up).astype(BF)
        gh = dh if scale is None else dh * scale
        gg = (gh * up * sig * (1.0 + gate * (1.0 - sig))).astype(BF)
        gu = (gh * gate * sig).astype(BF)
        return h, gg, gu

    lane16 = lax.broadcasted_iota(jnp.int32, (TOK, 128), 1)

    def stage_e(j):
        remote(got.at[j], got.at[j], rs_s.at[j], rs_r.at[j], sib).wait_recv()
        acc = part[j, px, py].astype(F32)
        for i in range(PEERS - 1):
            acc = acc + got[j, i].astype(F32)
        gate, up, dh = acc[:, 0:256], acc[:, 256:512], acc[:, 512:768]
        w = row_w[j, pl.ds(pl.multiple_of(px * TOK, TOK), TOK), :][:, 0:1]
        h, gg, gu = activations(gate, up, dh, w)
        s = jnp.sum(h.astype(F32) * dh, axis=1, keepdims=True)
        s_hi = s.astype(BF).astype(F32)
        tail = jnp.where(lane16 == 0, s_hi, jnp.where(lane16 == 1, s - s_hi, 0.0)).astype(BF)
        hid[j, dp] = jnp.concatenate((h, gg, gu, tail), axis=1)

        def send(i, carry):
            ag_copy(j, i).start()
            return carry

        lax.fori_loop(1, PEERS, send, 0)

    def ro_copy(j):
        return remote(rout.at[j, pl.ds(32, 32)], rsib.at[j], ro_s.at[j], ro_r.at[j], sib)

    def stage_m(j):
        many = hid.at[j, pl.ds(0, PEERS - 1)]
        remote(many, many, ag_s.at[j], ag_r.at[j], sib).wait_recv()

        def full(n):
            return jnp.concatenate(
                [
                    jnp.concatenate(
                        [hid[j, r * NY + u, :, n * 256 : n * 256 + 256] for u in range(NY)], axis=1
                    )
                    for r in range(NX)
                ],
                axis=0,
            )

        eo = dot_t(full(0), wd[...])
        rg = dot_t(full(1), wg[...]) + dot_t(full(2), wu[...])
        tails = []
        for r in range(NX):
            t = hid[j, r * NY, :, 768:896].astype(F32)
            for u in range(1, NY):
                t = t + hid[j, r * NY + u, :, 768:896].astype(F32)
            tails.append(t)
        s = jnp.sum(jnp.concatenate(tails, axis=0), axis=1, keepdims=True)
        s_hi = s.astype(BF).astype(F32)
        extra = row_m[j] * jnp.where(lane64 < 72, s_hi, s - s_hi)
        rout[j, :, 0:448] = (eo * row_w[j][:, 0:1]).astype(BF)
        rout[j, :, META:512] = (rout[j, :, META:512].astype(F32) + extra).astype(BF)
        rout[j, :, GRAD : GRAD + 448] = rg.astype(BF)
        ro_copy(j).start()

    def back_copy(key):
        d, k = key
        n = flat(key)
        p = BACK_PARENTS[d][k]
        return remote(
            back_out.at[n], back_in.at[n], rt_s.at[n], rt_r.at[n], z_dev(-sign[d] * (k - p))
        )

    def stage_c(j):
        ro_copy(j).wait_recv()
        both = jnp.concatenate((rout[j, 0:32], rsib[j]), axis=0)
        out = dot(pick[j][:, 0:64], both).reshape(8, TOK, WIDE)
        for i, (d, k) in enumerate(SLOTS[j]):
            if k not in BACKS[0]:
                back_out[j * 8 + i] = out[i].astype(BF)
                back_copy((d, k)).start()
            else:
                comb[j * 8 + i] = out[i]

    def children_sum(d, p, total):
        for k in BACKS[d].get(p, ()):
            back_copy((d, k)).wait_recv()
            total = total + back_in[flat((d, k))].astype(F32)
        return total

    def relay_out(k):
        for d in (0, 1):
            n = flat((d, k))
            back_out[n] = children_sum(d, k, comb[n]).astype(BF)
            back_copy((d, k)).start()

    def sr_copy(i):
        tx, ty = peer(i)
        return remote(s_part.at[tx * NY + ty], s_got.at[i - 1], rs_s.at[CHUNKS], rs_r.at[CHUNKS], peer_dev(i))

    def sa_copy(i):
        mine = s_hid.at[dp]
        return remote(mine, mine, ag_s.at[CHUNKS], ag_r.at[CHUNKS], peer_dev(i))

    def shared_p():
        for n, (x, w, load, mul) in enumerate(
            (
                (tokens[...], sg, loads[0], dot),
                (tokens[...], su, loads[1], dot),
                (own[:, GRAD : GRAD + 448], sd, loads[2], dot),
            )
        ):
            load.wait()
            val = mul(x, w[...]).astype(BF)
            for p in range(PEERS):
                s_part[p, :, n * 128 : n * 128 + 128] = val[:, p * 128 : p * 128 + 128]

        def send(i, carry):
            sr_copy(i).start()
            return carry

        lax.fori_loop(1, PEERS, send, 0)

    def shared_e():
        remote(s_got, s_got, rs_s.at[CHUNKS], rs_r.at[CHUNKS], sib).wait_recv()
        acc = s_part[dp].astype(F32)
        for i in range(PEERS - 1):
            acc = acc + s_got[i].astype(F32)
        h, gg, gu = activations(acc[:, 0:128], acc[:, 128:256], acc[:, 256:384], None)
        s_hid[dp] = jnp.concatenate((h, gg, gu), axis=1)

        def send(i, carry):
            sa_copy(i).start()
            return carry

        lax.fori_loop(1, PEERS, send, 0)

    def shared_m():
        many = s_hid.at[pl.ds(0, PEERS - 1)]
        remote(many, many, ag_s.at[CHUNKS], ag_r.at[CHUNKS], sib).wait_recv()

        def full(n):
            return jnp.concatenate([s_hid[p, :, n * 128 : n * 128 + 128] for p in range(PEERS)], axis=1)

        s_out[0] = dot_t(full(0), sd[...])
        s_out[1] = dot_t(full(1), sg[...]) + dot_t(full(2), su[...])

    forward(0, 0)
    forward(1, 0)
    shared_p()
    relay_in(4)
    stage_d(0)
    for load in loads[3:]:
        load.wait()
    stage_p(0)
    relay_in(8)
    stage_d(1)
    shared_e()
    stage_p(1)
    stage_e(0)
    relay_in(12)
    stage_d(2)
    stage_p(2)
    stage_e(1)
    stage_m(0)
    stage_d(3)
    stage_p(3)
    shared_m()
    stage_e(2)
    stage_c(0)
    stage_m(1)
    stage_e(3)
    stage_c(1)
    stage_m(2)
    stage_c(2)
    stage_m(3)
    stage_c(3)
    relay_out(12)
    relay_out(8)
    relay_out(4)
    total = children_sum(1, 0, children_sum(0, 0, comb[flat((0, 0))]))
    results[0:TOK] = s_out[0] + total[:, 0:448]
    results[TOK : 2 * TOK] = s_out[1] + total[:, GRAD : GRAD + 448]
    tail = total[:, META:512]
    results[2 * TOK :, 0:TOK] = dot_t(spread(64) + spread(72), tail.astype(BF))

    for j in range(CHUNKS):
        for i, key in enumerate(SLOTS[j]):
            if key != (0, 0):
                n = j * 8 + i
                remote(own, own, zs.at[n], zr.at[n], sib).wait_send()
                back_copy(key).wait_send()
        sib_copy(j).wait_send()
        ro_copy(j).wait_send()
        remote(got.at[j], got.at[j], rs_s.at[j], rs_r.at[j], sib).wait_send()
        many = hid.at[j, pl.ds(0, PEERS - 1)]
        remote(many, many, ag_s.at[j], ag_r.at[j], sib).wait_send()
    remote(s_got, s_got, rs_s.at[CHUNKS], rs_r.at[CHUNKS], sib).wait_send()
    many = s_hid.at[pl.ds(0, PEERS - 1)]
    remote(many, many, ag_s.at[CHUNKS], ag_r.at[CHUNKS], sib).wait_send()


def on_device(
    tokens, expert_ids, gate_weights, response_mask, cotangent,
    w_gate, w_up, w_down, shared_gate, shared_up, shared_down,
):
    vmem = pl.BlockSpec(memory_space=pltpu.VMEM)
    hbm = pl.BlockSpec(memory_space=pltpu.HBM)
    width = tokens.shape[1]
    units, shared_units = w_gate.shape[2], shared_gate.shape[1]
    sem = pltpu.SemaphoreType.DMA
    blocks = CHUNKS * 8
    results = pl.pallas_call(
        kernel,
        out_shape=jax.ShapeDtypeStruct((2 * TOK + TOP, width), F32),
        in_specs=[hbm] * 11,
        out_specs=vmem,
        scratch_shapes=[
            pltpu.VMEM((TOK, width), BF),
            pltpu.VMEM((TOP, TOK), jnp.int32),
            pltpu.VMEM((TOP, TOK), F32),
            pltpu.VMEM((1, TOK), jnp.int32),
            pltpu.VMEM((TOK, width), BF),
            pltpu.VMEM((width, units), BF),
            pltpu.VMEM((width, units), BF),
            pltpu.VMEM((width, units), BF),
            pltpu.VMEM((width, shared_units), BF),
            pltpu.VMEM((width, shared_units), BF),
            pltpu.VMEM((width, shared_units), BF),
            pltpu.VMEM((CHUNKS, 2, 8, TOK, WIDE), BF),
            pltpu.VMEM((CHUNKS, 128, 128), BF),
            pltpu.VMEM((CHUNKS, 64, 128), F32),
            pltpu.VMEM((CHUNKS, 64, 128), F32),
            pltpu.VMEM((CHUNKS, NX, NY, TOK, 768), BF),
            pltpu.VMEM((CHUNKS, PEERS - 1, TOK, 768), BF),
            pltpu.VMEM((CHUNKS, PEERS, TOK, 896), BF),
            pltpu.VMEM((CHUNKS, 64, WIDE), BF),
            pltpu.VMEM((CHUNKS, 32, WIDE), BF),
            pltpu.VMEM((blocks, TOK, WIDE), F32),
            pltpu.VMEM((blocks, TOK, WIDE), BF),
            pltpu.VMEM((blocks, TOK, WIDE), BF),
            pltpu.VMEM((PEERS, TOK, 384), BF),
            pltpu.VMEM((PEERS - 1, TOK, 384), BF),
            pltpu.VMEM((PEERS, TOK, 384), BF),
            pltpu.VMEM((2, TOK, width), F32),
            sem((11,)),
            sem((blocks,)),
            sem((blocks,)),
            sem((CHUNKS,)),
            sem((CHUNKS,)),
            sem((CHUNKS + 1,)),
            sem((CHUNKS + 1,)),
            sem((CHUNKS + 1,)),
            sem((CHUNKS + 1,)),
            sem((CHUNKS,)),
            sem((CHUNKS,)),
            sem((blocks,)),
            sem((blocks,)),
        ],
        compiler_params=pltpu.CompilerParams(
            collective_id=0, has_side_effects=True, vmem_limit_bytes=64 << 20
        ),
    )(
        tokens,
        expert_ids.T,
        gate_weights.T,
        response_mask.reshape(1, TOK),
        cotangent,
        w_gate[0],
        w_up[0],
        w_down[0].T,
        shared_gate,
        shared_up,
        shared_down.T,
    )
    return results[0:TOK].astype(BF), results[TOK : 2 * TOK].astype(BF), results[2 * TOK :, 0:TOK].T


def solution(mesh):
    return jax.shard_map(
        on_device,
        mesh=mesh,
        in_specs=(
            P("expert", "dp"),
            P("expert", None),
            P("expert", None),
            P("expert"),
            P("expert", "dp"),
            P("expert", "dp", None),
            P("expert", "dp", None),
            P("expert", None, "dp"),
            P("dp", None),
            P("dp", None),
            P(None, "dp"),
        ),
        out_specs=(P("expert", "dp"), P("expert", "dp"), P("expert", None)),
        check_vma=False,
    )
```

```python
import functools

import jax
import jax.numpy as jnp
from jax import lax
from jax.experimental import pallas as pl
from jax.experimental.pallas import tpu as pltpu
from jax.sharding import PartitionSpec as P

MESH = pl.DeviceIdType.MESH
BF = jnp.bfloat16
F32 = jnp.float32
NX, NY, NZ = 4, 4, 32
PEERS = NX * NY
CHUNKS = 4
CAP = 4
TOK = 16
TOP = 8
WIDE = 1024
GRAD = 512
META = 384

TREE_LONG = {0: (4, 2, 1), 4: (8, 6, 5, 3), 8: (12, 10, 9, 7), 12: (16, 15, 14, 13, 11)}
TREE_SHORT = {0: (4, 2, 1), 4: (8, 6, 5, 3), 8: (12, 10, 9, 7), 12: (15, 14, 13, 11)}
TREES = (TREE_LONG, TREE_SHORT)
PARENTS = tuple({k: p for p, ch in t.items() for k in ch} for t in TREES)
BACKS, BACK_PARENTS = TREES, PARENTS
HOPS = (1, 2, 3, 4)
SLOTS = (
    ((0, 0), (0, 1), (0, 2), (1, 1), (1, 2), (0, 4), (1, 4), (0, 3)),
    ((1, 3), (0, 5), (1, 5), (0, 6), (1, 6), (0, 8), (1, 8), (0, 7)),
    ((1, 7), (0, 9), (1, 9), (0, 10), (1, 10), (0, 12), (1, 12), (0, 11)),
    ((1, 11), (0, 13), (1, 13), (0, 14), (1, 14), (0, 15), (1, 15), (0, 16)),
)
PLACE = {key: (j, i) for j, row in enumerate(SLOTS) for i, key in enumerate(row)}


def flat(key):
    j, i = PLACE[key]
    return j * 8 + i


def dot(a, b):
    return lax.dot_general(a, b, (((1,), (0,)), ((), ())), preferred_element_type=F32)


def dot_t(a, b):
    return lax.dot_general(a, b, (((1,), (1,)), ((), ())), preferred_element_type=F32)


def t_dot(a, b):
    return lax.dot_general(a, b, (((0,), (0,)), ((), ())), preferred_element_type=F32)


def kernel(
    tokens_hbm, ids_hbm, weights_hbm, mask_hbm, cot_hbm, wg_hbm, wu_hbm, wd_hbm, sg_hbm, su_hbm, sd_hbm,
    results,
    tokens, ids, weights, mask, cot, wg, wu, wd, sg, su, sd,
    gath, pick, row_w, row_m, part, got, hid, rout, rsib, comb, back_out, back_in,
    s_part, s_got, s_hid, s_out,
    ld_sem, zs, zr, bs, br, rs_s, rs_r, ag_s, ag_r, ro_s, ro_r, rt_s, rt_r,
):
    dp = lax.axis_index("dp")
    ex = lax.axis_index("expert")
    z = ex // 2
    c = ex % 2
    px = dp // NY
    py = dp % NY
    sign = (1 - 2 * c, 2 * c - 1)

    def z_dev(dz):
        return (dp, lax.rem(z + dz + NZ, NZ) * 2 + c)

    sib = (dp, z * 2 + 1 - c)

    def peer(i):
        tx = lax.rem(px + i // NY, NX)
        ty = lax.rem(py + i % NY, NY)
        return tx, ty

    def peer_dev(i):
        tx, ty = peer(i)
        return (tx * NY + ty, ex)

    def remote(src, dst, ss, rs, dev):
        return pltpu.make_async_remote_copy(
            src_ref=src, dst_ref=dst, send_sem=ss, recv_sem=rs, device_id=dev, device_id_type=MESH
        )

    loads = [
        pltpu.make_async_copy(src, dst, ld_sem.at[n])
        for n, (src, dst) in enumerate(
            (
                (tokens_hbm, tokens), (ids_hbm, ids), (weights_hbm, weights), (mask_hbm, mask), (cot_hbm, cot),
                (sg_hbm, sg), (su_hbm, su), (sd_hbm, sd), (wg_hbm, wg), (wu_hbm, wu), (wd_hbm, wd),
            )
        )
    ]
    for load in loads:
        load.start()
    small, loads = loads[:5], loads[5:]

    barrier = pltpu.get_barrier_semaphore()
    pl.semaphore_signal(barrier, inc=1, device_id=sib, device_id_type=MESH)
    for h in HOPS:
        pl.semaphore_signal(barrier, inc=1, device_id=z_dev(h), device_id_type=MESH)
        pl.semaphore_signal(barrier, inc=1, device_id=z_dev(-h), device_id_type=MESH)

    def greet(i, carry):
        pl.semaphore_signal(barrier, inc=1, device_id=peer_dev(i), device_id_type=MESH)
        return carry

    lax.fori_loop(1, PEERS, greet, 0)

    lane = lax.broadcasted_iota(jnp.int32, (8, 128), 1)
    row = lax.broadcasted_iota(jnp.int32, (8, 128), 0)

    def spread(at):
        return jnp.where(lane == row + at, 1.0, 0.0).astype(BF)

    for load in small:
        load.wait()
    w_hi = weights[...].astype(BF)
    w_lo = (weights[...] - w_hi.astype(F32)).astype(BF)
    ids_b = ids[...].astype(F32).astype(BF)
    meta = t_dot(ids_b, spread(64) + spread(72)) + t_dot(w_hi, spread(80)) + t_dot(w_lo, spread(88))
    eye = lax.broadcasted_iota(jnp.int32, (TOK, TOK), 0) == lax.broadcasted_iota(jnp.int32, (TOK, TOK), 1)
    keep = jnp.where(eye, jnp.broadcast_to(mask[...].astype(F32), (TOK, TOK)), 0.0)
    grad = dot(keep.astype(BF), cot[...]).astype(BF)
    own = gath.at[PLACE[(0, 0)][0], c, PLACE[(0, 0)][1]]
    own[...] = jnp.zeros((TOK, WIDE), BF)
    own[:, 0:448] = tokens[...]
    own[:, META:512] = (own[:, META:512].astype(F32) + meta).astype(BF)
    own[:, GRAD : GRAD + 448] = grad
    rout[...] = jnp.zeros(rout.shape, BF)

    pl.semaphore_wait(barrier, PEERS + 2 * len(HOPS))

    def z_copy(key, child):
        j, i = PLACE[key]
        jj, ii = PLACE[child]
        n = flat(child)
        d, k = child
        return remote(
            gath.at[j, c, i], gath.at[jj, c, ii], zs.at[n], zr.at[n], z_dev(sign[d] * (k - key[1]))
        )

    def forward(d, p):
        for k in TREES[d].get(p, ()):
            z_copy((0, 0) if p == 0 else (d, p), (d, k)).start()

    def arrive(key):
        d, k = key
        p = PARENTS[d][k]
        z_copy((0, 0) if p == 0 else (d, p), key).wait_recv()
        forward(d, k)

    def sib_copy(j):
        return remote(gath.at[j, c], gath.at[j, c], bs.at[j], br.at[j], sib)

    def relay_in(k):
        arrive((0, k))
        arrive((1, k))

    def stage_d(j):
        for d, k in SLOTS[j]:
            if k in (0, 4, 8, 12):
                continue
            arrive((d, k))
        sib_copy(j).start()

    tok_row = lax.broadcasted_iota(jnp.int32, (128, 128), 0)
    tok_lane = lax.broadcasted_iota(jnp.int32, (128, 128), 1)
    lower = jnp.where((tok_lane < tok_row) & (tok_lane // TOK == tok_row // TOK), 1.0, 0.0).astype(BF)
    ones = jnp.ones((128, 128), BF)
    base = (tok_row // TOK) * CAP

    def selector(meta_f, expert, at):
        match = (tok_lane >= 64) & (tok_lane < 72) & (meta_f == expert)
        hit = dot(jnp.where(match, 1.0, 0.0).astype(BF), ones)
        pos = dot(lower, hit.astype(BF))
        here = (hit > 0.5) & (tok_lane.astype(F32) == (base + at).astype(F32) + pos)
        return jnp.where(here, 1.0, 0.0)

    e_own = ex.astype(F32)
    e_sib = (z * 2 + 1 - c).astype(F32)
    lane64 = lax.broadcasted_iota(jnp.int32, (64, 128), 1)

    def rs_copy(j, i):
        tx, ty = peer(i)
        return remote(part.at[j, tx, ty], got.at[j, i - 1], rs_s.at[j], rs_r.at[j], peer_dev(i))

    def stage_p(j):
        sib_copy(j).wait_recv()
        toks_c = gath[j, c].reshape(128, WIDE)
        toks_s = gath[j, 1 - c].reshape(128, WIDE)
        meta_c = toks_c[:, META:512].astype(F32)
        meta_s = toks_s[:, META:512].astype(F32)
        sel_c = selector(meta_c, e_own, 0)
        sel_s = selector(meta_s, e_own, 0)
        pick[j] = (sel_c + selector(meta_c, e_sib, 32)).astype(BF)
        rows_c = dot(sel_c.T[0:32].astype(BF), toks_c)
        rows_s = dot(sel_s.T[0:32].astype(BF), toks_s)
        rows = jnp.concatenate((rows_c, rows_s), axis=0)
        rmeta = rows[:, META:512]
        same = rmeta == e_own
        both = pltpu.roll(rmeta, 112, 1) + pltpu.roll(rmeta, 104, 1)
        w = jnp.sum(jnp.where(same & (lane64 >= 64) & (lane64 < 72), both, 0.0), axis=1, keepdims=True)
        row_w[j] = jnp.broadcast_to(w, (64, 128))
        row_m[j] = jnp.where(same & (lane64 >= 64) & (lane64 < 80), 1.0, 0.0)
        rows = rows.astype(BF)
        x = rows[:, 0:448]
        g = rows[:, GRAD : GRAD + 448]
        for n, val in enumerate((dot(x, wg[...]), dot(x, wu[...]), dot(g, wd[...]))):
            val = val.astype(BF).reshape(NX, TOK, 1024)
            for u in range(NY):
                part[j, :, u, :, n * 256 : n * 256 + 256] = val[:, :, u * 256 : u * 256 + 256]

        def send(i, carry):
            rs_copy(j, i).start()
            return carry

        lax.fori_loop(1, PEERS, send, 0)

    def ag_copy(j, i):
        mine = hid.at[j, dp]
        return remote(mine, mine, ag_s.at[j], ag_r.at[j], peer_dev(i))

    def activations(gate, up, dh, scale):
        sig = jax.nn.sigmoid(gate)
        h = (gate * sig * up).astype(BF)
        gh = dh if scale is None else dh * scale
        gg = (gh * up * sig * (1.0 + gate * (1.0 - sig))).astype(BF)
        gu = (gh * gate * sig).astype(BF)
        return h, gg, gu

    lane16 = lax.broadcasted_iota(jnp.int32, (TOK, 128), 1)

    def stage_e(j):
        remote(got.at[j], got.at[j], rs_s.at[j], rs_r.at[j], sib).wait_recv()
        acc = part[j, px, py].astype(F32)
        for i in range(PEERS - 1):
            acc = acc + got[j, i].astype(F32)
        gate, up, dh = acc[:, 0:256], acc[:, 256:512], acc[:, 512:768]
        w = row_w[j, pl.ds(pl.multiple_of(px * TOK, TOK), TOK), :][:, 0:1]
        h, gg, gu = activations(gate, up, dh, w)
        s = jnp.sum(h.astype(F32) * dh, axis=1, keepdims=True)
        s_hi = s.astype(BF).astype(F32)
        tail = jnp.where(lane16 == 0, s_hi, jnp.where(lane16 == 1, s - s_hi, 0.0)).astype(BF)
        hid[j, dp] = jnp.concatenate((h, gg, gu, tail), axis=1)

        def send(i, carry):
            ag_copy(j, i).start()
            return carry

        lax.fori_loop(1, PEERS, send, 0)

    def ro_copy(j):
        return remote(rout.at[j, pl.ds(32, 32)], rsib.at[j], ro_s.at[j], ro_r.at[j], sib)

    def stage_m(j):
        many = hid.at[j, pl.ds(0, PEERS - 1)]
        remote(many, many, ag_s.at[j], ag_r.at[j], sib).wait_recv()

        def full(n):
            return jnp.concatenate(
                [
                    jnp.concatenate(
                        [hid[j, r * NY + u, :, n * 256 : n * 256 + 256] for u in range(NY)], axis=1
                    )
                    for r in range(NX)
                ],
                axis=0,
            )

        eo = dot_t(full(0), wd[...])
        rg = dot_t(full(1), wg[...]) + dot_t(full(2), wu[...])
        tails = []
        for r in range(NX):
            t = hid[j, r * NY, :, 768:896].astype(F32)
            for u in range(1, NY):
                t = t + hid[j, r * NY + u, :, 768:896].astype(F32)
            tails.append(t)
        s = jnp.sum(jnp.concatenate(tails, axis=0), axis=1, keepdims=True)
        s_hi = s.astype(BF).astype(F32)
        extra = row_m[j] * jnp.where(lane64 < 72, s_hi, s - s_hi)
        rout[j, :, 0:448] = (eo * row_w[j][:, 0:1]).astype(BF)
        rout[j, :, META:512] = (rout[j, :, META:512].astype(F32) + extra).astype(BF)
        rout[j, :, GRAD : GRAD + 448] = rg.astype(BF)
        ro_copy(j).start()

    def back_copy(key):
        d, k = key
        n = flat(key)
        p = BACK_PARENTS[d][k]
        return remote(
            back_out.at[n], back_in.at[n], rt_s.at[n], rt_r.at[n], z_dev(-sign[d] * (k - p))
        )

    def stage_c(j):
        ro_copy(j).wait_recv()
        both = jnp.concatenate((rout[j, 0:32], rsib[j]), axis=0)
        out = dot(pick[j][:, 0:64], both).reshape(8, TOK, WIDE)
        for i, (d, k) in enumerate(SLOTS[j]):
            if k not in BACKS[0]:
                back_out[j * 8 + i] = out[i].astype(BF)
                back_copy((d, k)).start()
            else:
                comb[j * 8 + i] = out[i]

    def children_sum(d, p, total):
        for k in BACKS[d].get(p, ()):
            back_copy((d, k)).wait_recv()
            total = total + back_in[flat((d, k))].astype(F32)
        return total

    def relay_out(k):
        for d in (0, 1):
            n = flat((d, k))
            back_out[n] = children_sum(d, k, comb[n]).astype(BF)
            back_copy((d, k)).start()

    def sr_copy(i):
        tx, ty = peer(i)
        return remote(s_part.at[tx * NY + ty], s_got.at[i - 1], rs_s.at[CHUNKS], rs_r.at[CHUNKS], peer_dev(i))

    def sa_copy(i):
        mine = s_hid.at[dp]
        return remote(mine, mine, ag_s.at[CHUNKS], ag_r.at[CHUNKS], peer_dev(i))

    def shared_p():
        for n, (x, w, load, mul) in enumerate(
            (
                (tokens[...], sg, loads[0], dot),
                (tokens[...], su, loads[1], dot),
                (own[:, GRAD : GRAD + 448], sd, loads[2], dot),
            )
        ):
            load.wait()
            val = mul(x, w[...]).astype(BF)
            for p in range(PEERS):
                s_part[p, :, n * 128 : n * 128 + 128] = val[:, p * 128 : p * 128 + 128]

        def send(i, carry):
            sr_copy(i).start()
            return carry

        lax.fori_loop(1, PEERS, send, 0)

    def shared_e():
        remote(s_got, s_got, rs_s.at[CHUNKS], rs_r.at[CHUNKS], sib).wait_recv()
        acc = s_part[dp].astype(F32)
        for i in range(PEERS - 1):
            acc = acc + s_got[i].astype(F32)
        h, gg, gu = activations(acc[:, 0:128], acc[:, 128:256], acc[:, 256:384], None)
        s_hid[dp] = jnp.concatenate((h, gg, gu), axis=1)

        def send(i, carry):
            sa_copy(i).start()
            return carry

        lax.fori_loop(1, PEERS, send, 0)

    def shared_m():
        many = s_hid.at[pl.ds(0, PEERS - 1)]
        remote(many, many, ag_s.at[CHUNKS], ag_r.at[CHUNKS], sib).wait_recv()

        def full(n):
            return jnp.concatenate([s_hid[p, :, n * 128 : n * 128 + 128] for p in range(PEERS)], axis=1)

        s_out[0] = dot_t(full(0), sd[...])
        s_out[1] = dot_t(full(1), sg[...]) + dot_t(full(2), su[...])

    forward(0, 0)
    forward(1, 0)
    shared_p()
    relay_in(4)
    stage_d(0)
    for load in loads[3:]:
        load.wait()
    stage_p(0)
    relay_in(8)
    stage_d(1)
    shared_e()
    stage_p(1)
    stage_e(0)
    relay_in(12)
    stage_d(2)
    stage_p(2)
    stage_e(1)
    stage_d(3)
    stage_p(3)
    stage_m(0)
    stage_e(2)
    stage_c(0)
    stage_e(3)
    stage_m(1)
    stage_c(1)
    stage_m(2)
    shared_m()
    stage_c(2)
    stage_m(3)
    stage_c(3)
    relay_out(12)
    relay_out(8)
    relay_out(4)
    total = children_sum(1, 0, children_sum(0, 0, comb[flat((0, 0))]))
    results[0:TOK] = s_out[0] + total[:, 0:448]
    results[TOK : 2 * TOK] = s_out[1] + total[:, GRAD : GRAD + 448]
    tail = total[:, META:512]
    results[2 * TOK :, 0:TOK] = dot_t(spread(64) + spread(72), tail.astype(BF))

    for j in range(CHUNKS):
        for i, key in enumerate(SLOTS[j]):
            if key != (0, 0):
                n = j * 8 + i
                remote(own, own, zs.at[n], zr.at[n], sib).wait_send()
                back_copy(key).wait_send()
        sib_copy(j).wait_send()
        ro_copy(j).wait_send()
        remote(got.at[j], got.at[j], rs_s.at[j], rs_r.at[j], sib).wait_send()
        many = hid.at[j, pl.ds(0, PEERS - 1)]
        remote(many, many, ag_s.at[j], ag_r.at[j], sib).wait_send()
    remote(s_got, s_got, rs_s.at[CHUNKS], rs_r.at[CHUNKS], sib).wait_send()
    many = s_hid.at[pl.ds(0, PEERS - 1)]
    remote(many, many, ag_s.at[CHUNKS], ag_r.at[CHUNKS], sib).wait_send()


def on_device(
    tokens, expert_ids, gate_weights, response_mask, cotangent,
    w_gate, w_up, w_down, shared_gate, shared_up, shared_down,
):
    vmem = pl.BlockSpec(memory_space=pltpu.VMEM)
    hbm = pl.BlockSpec(memory_space=pltpu.HBM)
    width = tokens.shape[1]
    units, shared_units = w_gate.shape[2], shared_gate.shape[1]
    sem = pltpu.SemaphoreType.DMA
    blocks = CHUNKS * 8
    results = pl.pallas_call(
        kernel,
        out_shape=jax.ShapeDtypeStruct((2 * TOK + TOP, width), F32),
        in_specs=[hbm] * 11,
        out_specs=vmem,
        scratch_shapes=[
            pltpu.VMEM((TOK, width), BF),
            pltpu.VMEM((TOP, TOK), jnp.int32),
            pltpu.VMEM((TOP, TOK), F32),
            pltpu.VMEM((1, TOK), jnp.int32),
            pltpu.VMEM((TOK, width), BF),
            pltpu.VMEM((width, units), BF),
            pltpu.VMEM((width, units), BF),
            pltpu.VMEM((width, units), BF),
            pltpu.VMEM((width, shared_units), BF),
            pltpu.VMEM((width, shared_units), BF),
            pltpu.VMEM((width, shared_units), BF),
            pltpu.VMEM((CHUNKS, 2, 8, TOK, WIDE), BF),
            pltpu.VMEM((CHUNKS, 128, 128), BF),
            pltpu.VMEM((CHUNKS, 64, 128), F32),
            pltpu.VMEM((CHUNKS, 64, 128), F32),
            pltpu.VMEM((CHUNKS, NX, NY, TOK, 768), BF),
            pltpu.VMEM((CHUNKS, PEERS - 1, TOK, 768), BF),
            pltpu.VMEM((CHUNKS, PEERS, TOK, 896), BF),
            pltpu.VMEM((CHUNKS, 64, WIDE), BF),
            pltpu.VMEM((CHUNKS, 32, WIDE), BF),
            pltpu.VMEM((blocks, TOK, WIDE), F32),
            pltpu.VMEM((blocks, TOK, WIDE), BF),
            pltpu.VMEM((blocks, TOK, WIDE), BF),
            pltpu.VMEM((PEERS, TOK, 384), BF),
            pltpu.VMEM((PEERS - 1, TOK, 384), BF),
            pltpu.VMEM((PEERS, TOK, 384), BF),
            pltpu.VMEM((2, TOK, width), F32),
            sem((11,)),
            sem((blocks,)),
            sem((blocks,)),
            sem((CHUNKS,)),
            sem((CHUNKS,)),
            sem((CHUNKS + 1,)),
            sem((CHUNKS + 1,)),
            sem((CHUNKS + 1,)),
            sem((CHUNKS + 1,)),
            sem((CHUNKS,)),
            sem((CHUNKS,)),
            sem((blocks,)),
            sem((blocks,)),
        ],
        compiler_params=pltpu.CompilerParams(
            collective_id=0, has_side_effects=True, vmem_limit_bytes=64 << 20
        ),
    )(
        tokens,
        expert_ids.T,
        gate_weights.T,
        response_mask.reshape(1, TOK),
        cotangent,
        w_gate[0],
        w_up[0],
        w_down[0].T,
        shared_gate,
        shared_up,
        shared_down.T,
    )
    return results[0:TOK].astype(BF), results[TOK : 2 * TOK].astype(BF), results[2 * TOK :, 0:TOK].T


def solution(mesh):
    return jax.shard_map(
        on_device,
        mesh=mesh,
        in_specs=(
            P("expert", "dp"),
            P("expert", None),
            P("expert", None),
            P("expert"),
            P("expert", "dp"),
            P("expert", "dp", None),
            P("expert", "dp", None),
            P("expert", None, "dp"),
            P("dp", None),
            P("dp", None),
            P(None, "dp"),
        ),
        out_specs=(P("expert", "dp"), P("expert", "dp"), P("expert", None)),
        check_vma=False,
    )
```
